256 devices in a mesh: dp: 64 (over x, y, z_lo), mp: 4 (over z_hi, core).
Axes of the slice: x: 4, y: 4, z: 8 (z_hi: 2, z_lo: 4; z = z_hi * 4 + z_lo), core: 2. Of those that a mesh axis runs over, the one named last changes fastest.
Arguments:
- grad: bfloat16 [16384, 8192], P('dp', 'mp'), may hold values from -6 to 6
- right_basis: bfloat16 [8, 1024, 1024], P('mp', 'dp'), may hold values from -0.1875 to 0.1875
- left_basis: bfloat16 [16, 1024, 1024], P('mp', 'dp'), may hold values from -0.1875 to 0.1875
- first_moment: float32 [16384, 8192], P('mp', 'dp'), may hold values from -6 to 6
- second_moment: float32 [16384, 8192], P('mp', 'dp'), may hold values from 0.1 to 10
Outputs:
- update: float32 [16384, 8192], P('dp', 'mp')
- first_new: float32 [16384, 8192], P('mp', 'dp')
- second_new: float32 [16384, 8192], P('mp', 'dp')
The draws below stay inside these ranges and needn't reach their ends.
All inputs are finite; a program needn't handle non-finite values.
Results may differ from the reference program's by a relative error of at most 0.0041.
Values may be sent and summed in bfloat16 or wider, within the bound.
No kernel may reach another device: no remote copies, remote signals or barrier semaphores. Data moves between devices by JAX's collectives and lax.ppermute only.
A program may use at most 64 MiB of HBM per device.

```python
import math
import jax
import jax.numpy as jnp

WIDTH = 8192
HIDDEN_SIZE = 16384
BLOCK = 1024
COL_BLOCKS = 8
ROW_BLOCKS = 16
N_DP = 64
N_MP = 4


def steps_of(own_key, shape, shards, least, top_value):
    level, own = 1.0, jax.random.fold_in(own_key, 6)
    for axis_at, blocks in shards:
        draws = jnp.exp(jax.random.uniform(jax.random.fold_in(own, axis_at), (blocks,), jnp.float32, least / len(shards), top_value / len(shards)))
        level = level * jnp.repeat(draws, shape[axis_at] // blocks).reshape([-1 if axis == axis_at else 1 for axis in range(len(shape))])
    return level


def noise(stream_key, extent, width, bound, split=(), dtype=jnp.bfloat16):
    values = width * jax.random.normal(stream_key, extent, jnp.float32)
    if split:
        values = values * steps_of(stream_key, extent, split, -0.22, 0.18)
    return jnp.clip(values, -bound, bound).astype(dtype)


def setup_inputs(seed: int = 0) -> dict:
    streams_of = jax.random.split(jax.random.key(seed), 6)
    return {
        "grad": noise(streams_of[0], (HIDDEN_SIZE, WIDTH), 1.0, 6.0, ((0, 64), (1, 4))),
        "right_basis": noise(streams_of[1], (COL_BLOCKS, BLOCK, BLOCK), BLOCK ** -0.5, 0.1875, ((0, 4), (1, 64))),
        "left_basis": noise(streams_of[2], (ROW_BLOCKS, BLOCK, BLOCK), BLOCK ** -0.5, 0.1875, ((0, 4), (1, 64))),
        "first_moment": noise(streams_of[3], (HIDDEN_SIZE, WIDTH), 1.0, 6.0, ((0, 4), (1, 64)), jnp.float32),
        "second_moment": jnp.clip(jnp.exp(math.log(10.0) - 4.6051702 * jax.random.uniform(streams_of[4], (HIDDEN_SIZE, WIDTH), jnp.float32) ** steps_of(streams_of[4], (HIDDEN_SIZE, WIDTH), ((0, 4), (1, 64)), -0.2, 0.2)), 0.1, 10.0),
    }


beta_one = 0.95
beta_two = 0.95
bias_one = 1.0 - 0.95 ** 10
bias_two = 1.0 - 0.95 ** 10
epsilon = 1e-08

def reference(grad, right_basis, left_basis, first_moment, second_moment):
    column_blocks = WIDTH // BLOCK
    row_blocks = HIDDEN_SIZE // BLOCK
    piece_width = WIDTH // (N_MP * N_DP)
    grad_blocks = grad.astype(jnp.float32).reshape(HIDDEN_SIZE, column_blocks, BLOCK)
    rotated_cols = jnp.einsum('rki,kio->rko', grad_blocks, right_basis.astype(jnp.float32))
    rotated_cols = rotated_cols.reshape(HIDDEN_SIZE, WIDTH).astype(jnp.bfloat16)
    owned = rotated_cols.astype(jnp.float32).reshape(row_blocks, BLOCK, WIDTH)
    rotated = jnp.einsum('bio,bic->boc', left_basis.astype(jnp.float32), owned).reshape(HIDDEN_SIZE, WIDTH)
    eigen_grad = rotated.reshape(HIDDEN_SIZE, N_MP, N_DP, piece_width).transpose(0, 2, 1, 3).reshape(HIDDEN_SIZE, WIDTH)
    first_new = beta_one * first_moment + (1.0 - beta_one) * eigen_grad
    second_new = beta_two * second_moment + (1.0 - beta_two) * eigen_grad * eigen_grad
    direction = (first_new / bias_one / (jnp.sqrt(second_new / bias_two) + epsilon)).astype(jnp.bfloat16)
    back_order = direction.reshape(HIDDEN_SIZE, N_DP, N_MP, piece_width).transpose(0, 2, 1, 3).reshape(HIDDEN_SIZE, WIDTH)
    back_blocks = back_order.astype(jnp.float32).reshape(row_blocks, BLOCK, WIDTH)
    back_rows = jnp.einsum('bio,boc->bic', left_basis.astype(jnp.float32), back_blocks)
    back_rows = back_rows.reshape(HIDDEN_SIZE, WIDTH).astype(jnp.bfloat16)
    back_cols = back_rows.astype(jnp.float32).reshape(HIDDEN_SIZE, column_blocks, BLOCK)
    update = jnp.einsum('rko,kio->rki', back_cols, right_basis.astype(jnp.float32)).reshape(HIDDEN_SIZE, WIDTH)
    return (update, first_new, second_new)
```

```python
import jax
import jax.numpy as jnp
from jax import lax
from jax.sharding import Mesh, PartitionSpec as P

beta_one = 0.95
beta_two = 0.95
bias_one = 1.0 - 0.95**10
bias_two = 1.0 - 0.95**10
epsilon = 1e-08

XY = ("x", "y")
ZC = ("zl", "zh", "core")


def gather_basis(shard):
    blocks, rows, width = shard.shape
    line = lax.all_gather(shard.reshape(blocks * rows, width), "zl", axis=0, tiled=True)
    whole = lax.all_gather(line, XY, axis=0, tiled=True)
    whole = whole.reshape(64, blocks, rows, width).transpose(1, 0, 2, 3)
    return whole.reshape(blocks, 64 * rows, width)


def on_device(grad, right_basis, left_basis, first_moment, second_moment):
    right_whole = gather_basis(right_basis)
    left_whole = gather_basis(left_basis)
    turned = jnp.einsum(
        "rki,kio->kor",
        grad.reshape(256, 2, 1024),
        right_whole,
        preferred_element_type=jnp.float32,
    ).astype(jnp.bfloat16)
    sent = turned.reshape(16, 128, 256)
    crossed = lax.all_to_all(sent, XY, split_axis=0, concat_axis=0, tiled=True)
    pieces = crossed.reshape(4, 4, 4, 32, 256).transpose(2, 0, 1, 3, 4).reshape(16, 128, 256)
    owned = lax.all_to_all(pieces, ZC, split_axis=0, concat_axis=0, tiled=True)
    owned = owned.reshape(4, 4, 4, 32, 256).transpose(2, 1, 3, 0, 4).reshape(4, 128, 1024)
    eigen_grad = jnp.einsum(
        "bio,bci->boc", left_whole, owned, preferred_element_type=jnp.float32
    ).reshape(4096, 128)
    first_new = beta_one * first_moment + (1.0 - beta_one) * eigen_grad
    second_new = beta_two * second_moment + (1.0 - beta_two) * eigen_grad * eigen_grad
    direction = (first_new / bias_one / (jnp.sqrt(second_new / bias_two) + epsilon)).astype(
        jnp.bfloat16
    )
    back = jnp.einsum(
        "bio,boc->bci",
        left_whole,
        direction.reshape(4, 1024, 128),
        preferred_element_type=jnp.float32,
    ).astype(jnp.bfloat16)
    back = back.reshape(4, 4, 32, 4, 256).transpose(3, 1, 0, 2, 4).reshape(16, 128, 256)
    back = lax.all_to_all(back, ZC, split_axis=0, concat_axis=0, tiled=True)
    back = back.reshape(4, 4, 4, 32, 256).transpose(1, 2, 0, 3, 4).reshape(16, 128, 256)
    back = lax.all_to_all(back, XY, split_axis=0, concat_axis=0, tiled=True)
    update = jnp.einsum(
        "kor,kio->rki",
        back.reshape(2, 1024, 256),
        right_whole,
        preferred_element_type=jnp.float32,
    )
    return update.reshape(256, 2048), first_new, second_new


def solution(mesh):
    fine = Mesh(mesh.devices.reshape(4, 4, 4, 2, 2), ("x", "y", "zl", "zh", "core"))
    dp, mp = ("x", "y", "zl"), ("zh", "core")
    in_specs = (P(dp, mp), P(mp, dp, None), P(mp, dp, None), P(mp, dp), P(mp, dp))
    out_specs = (P(dp, mp), P(mp, dp), P(mp, dp))
    return jax.shard_map(
        on_device, mesh=fine, in_specs=in_specs, out_specs=out_specs, check_vma=False
    )
```

```python
import jax
import jax.numpy as jnp
from jax import lax
from jax.experimental import pallas as pl
from jax.experimental.pallas import tpu as pltpu
from jax.sharding import Mesh, PartitionSpec as P

beta_one = 0.95
beta_two = 0.95
bias_one = 1.0 - 0.95**10
bias_two = 1.0 - 0.95**10
epsilon = 1e-08

XY = ("x", "y")
ZC = ("zl", "zh", "core")
NEAR = (0, -1, 1, 2)
BLOCK = 1024
ROWS = 256
VMEM_LIMIT = 32 * 1024 * 1024


def shift(value, axis, by):
    return lax.ppermute(value, axis, [(i, (i + by) % 4) for i in range(4)])


def line_gather(shard, zl):
    held = [shard] + [shift(shard, "zl", t) for t in (1, 2, 3)]
    ordered = []
    for at in range(4):
        back = (zl - at) & 3
        ordered.append(
            jnp.where(
                back < 2,
                jnp.where(back == 0, held[0], held[1]),
                jnp.where(back == 2, held[2], held[3]),
            )
        )
    return jnp.stack(ordered, axis=-3).reshape(*shard.shape[:-2], 64, BLOCK)


def rings(first, second, first_axis, second_axis):
    pairs = [(first, second)]
    for by in (1, -1, 2):
        pairs.append((shift(first, first_axis, by), shift(second, second_axis, by)))
    return [pair[0] for pair in pairs], [pair[1] for pair in pairs]


def chip_row(place, half, outer, inner):
    to_x, to_y = (inner, outer) if half == 0 else (outer, inner)
    chip = ((place[0] + to_x + 4) & 3) * 4 + ((place[1] + to_y + 4) & 3)
    return pl.multiple_of(chip * 64, 64)


def first_kernel(place, grad, *refs):
    pieces, (sent, right_whole) = refs[:8], refs[8:]

    for k in range(2):

        @pl.when(pl.program_id(0) == k)
        def _():
            for piece in range(4):
                for at in range(4):
                    row = chip_row(place, k, NEAR[piece], NEAR[at])
                    right_whole[0, pl.ds(row, 64), :] = pieces[4 * k + piece][at]

    turned = jnp.dot(grad[...], right_whole[0], preferred_element_type=jnp.float32)
    sent[...] = turned.astype(jnp.bfloat16).T.reshape(8, 128, ROWS)


def first_stage(place, grad, pieces):
    return pl.pallas_call(
        first_kernel,
        out_shape=(
            jax.ShapeDtypeStruct((16, 128, ROWS), jnp.bfloat16),
            jax.ShapeDtypeStruct((2, BLOCK, BLOCK), jnp.bfloat16),
        ),
        grid_spec=pltpu.PrefetchScalarGridSpec(
            num_scalar_prefetch=1,
            grid=(2,),
            in_specs=[pl.BlockSpec((ROWS, BLOCK), lambda k, place: (0, k))]
            + [pl.BlockSpec((4, 64, BLOCK), lambda k, place: (0, 0, 0))] * len(pieces),
            out_specs=(
                pl.BlockSpec((8, 128, ROWS), lambda k, place: (k, 0, 0)),
                pl.BlockSpec((1, BLOCK, BLOCK), lambda k, place: (k, 0, 0)),
            ),
        ),
        compiler_params=pltpu.CompilerParams(vmem_limit_bytes=VMEM_LIMIT),
        cost_estimate=pl.CostEstimate(
            flops=2 * ROWS * 2 * BLOCK * BLOCK, bytes_accessed=10 * 2**20, transcendentals=0
        ),
        name="rotate_columns",
    )(place, grad, *pieces)


def middle_kernel(owned, left_block, first, second, back, first_out, second_out):
    left = left_block[:, 0].reshape(BLOCK, BLOCK)
    columns = jnp.concatenate(
        [owned[4 * z : 4 * z + 4, 0].reshape(128, ROWS) for z in range(4)], axis=1
    )
    eigen_grad = jnp.dot(columns, left, preferred_element_type=jnp.float32).T
    first_new = beta_one * first[...] + (1.0 - beta_one) * eigen_grad
    second_new = beta_two * second[...] + (1.0 - beta_two) * eigen_grad * eigen_grad
    first_out[...] = first_new
    second_out[...] = second_new
    direction = first_new / bias_one / (jnp.sqrt(second_new / bias_two) + epsilon)
    turned = lax.dot_general(
        direction.astype(jnp.bfloat16).T,
        left,
        (((1,), (1,)), ((), ())),
        preferred_element_type=jnp.float32,
    ).astype(jnp.bfloat16)
    for z in range(4):
        back[4 * z : 4 * z + 4, 0] = turned[:, z * ROWS : (z + 1) * ROWS].reshape(4, 32, ROWS)


def middle_stage(owned, left_whole, first_moment, second_moment):
    pieces = pl.BlockSpec((16, 1, 32, ROWS), lambda b: (0, b, 0, 0))
    moments = pl.BlockSpec((BLOCK, 128), lambda b: (b, 0))
    return pl.pallas_call(
        middle_kernel,
        out_shape=(
            jax.ShapeDtypeStruct((16, 4, 32, ROWS), jnp.bfloat16),
            jax.ShapeDtypeStruct((4 * BLOCK, 128), jnp.float32),
            jax.ShapeDtypeStruct((4 * BLOCK, 128), jnp.float32),
        ),
        grid=(4,),
        in_specs=[
            pieces,
            pl.BlockSpec((16, 1, 64, BLOCK), lambda b: (0, b, 0, 0)),
            moments,
            moments,
        ],
        out_specs=(pieces, moments, moments),
        compiler_params=pltpu.CompilerParams(vmem_limit_bytes=VMEM_LIMIT),
        cost_estimate=pl.CostEstimate(
            flops=4 * 4 * BLOCK * BLOCK * 128,
            bytes_accessed=18 * 2**20,
            transcendentals=4 * BLOCK * 128,
        ),
        name="moments_and_direction",
    )(owned, left_whole, first_moment, second_moment)


def last_kernel(back, right_whole, update):
    update[...] = lax.dot_general(
        back[...].reshape(BLOCK, ROWS).T,
        right_whole[0],
        (((1,), (1,)), ((), ())),
        preferred_element_type=jnp.float32,
    )


def last_stage(back, right_whole):
    return pl.pallas_call(
        last_kernel,
        out_shape=jax.ShapeDtypeStruct((ROWS, 2 * BLOCK), jnp.float32),
        grid=(2, 2),
        in_specs=[
            pl.BlockSpec((8, 128, ROWS), lambda k, i: (k, 0, 0)),
            pl.BlockSpec((1, BLOCK // 2, BLOCK), lambda k, i: (k, i, 0)),
        ],
        out_specs=pl.BlockSpec((ROWS, BLOCK // 2), lambda k, i: (0, 2 * k + i)),
        compiler_params=pltpu.CompilerParams(vmem_limit_bytes=VMEM_LIMIT),
        cost_estimate=pl.CostEstimate(
            flops=2 * ROWS * 2 * BLOCK * BLOCK, bytes_accessed=7 * 2**20, transcendentals=0
        ),
        name="rotate_back_columns",
    )(back, right_whole)


def on_device(grad, right_basis, left_basis, first_moment, second_moment):
    place = jnp.stack([lax.axis_index(axis) for axis in ("x", "y", "zl")]).astype(jnp.int32)
    zl = place[2]
    line = line_gather(jnp.concatenate([right_basis, left_basis]), zl)
    left_whole = lax.all_gather(line[2:].reshape(256, BLOCK), XY, axis=0, tiled=True)
    left_whole = left_whole.reshape(16, 4, 64, BLOCK)
    right_x, right_y = rings(line[0], line[1], "x", "y")
    right_x, right_y = lax.optimization_barrier((jnp.stack(right_x), jnp.stack(right_y)))
    right_x, right_y = rings(right_x, right_y, "y", "x")
    sent, right_whole = first_stage(place, grad, right_x + right_y)
    crossed = lax.all_to_all(sent, XY, split_axis=0, concat_axis=0, tiled=True)
    crossed = crossed.reshape(4, 4, 4, 32, ROWS).transpose(2, 0, 1, 3, 4).reshape(16, 128, ROWS)
    owned = lax.all_to_all(crossed, ZC, split_axis=0, concat_axis=0, tiled=True)
    left_whole, first_moment, second_moment = (
        pltpu.with_memory_space_constraint(value, pltpu.HBM)
        for value in (left_whole, first_moment, second_moment)
    )
    back, first_new, second_new = middle_stage(
        owned.reshape(16, 4, 32, ROWS), left_whole, first_moment, second_moment
    )
    back = lax.all_to_all(
        back.reshape(16, 128, ROWS), ZC, split_axis=0, concat_axis=0, tiled=True
    )
    back = back.reshape(4, 4, 4, 32, ROWS).transpose(1, 2, 0, 3, 4).reshape(16, 128, ROWS)
    back = lax.all_to_all(back, XY, split_axis=0, concat_axis=0, tiled=True)
    return last_stage(back, right_whole), first_new, second_new


def solution(mesh):
    fine = Mesh(mesh.devices.reshape(4, 4, 4, 2, 2), ("x", "y", "zl", "zh", "core"))
    dp, mp = ("x", "y", "zl"), ("zh", "core")
    in_specs = (P(dp, mp), P(mp, dp, None), P(mp, dp, None), P(mp, dp), P(mp, dp))
    out_specs = (P(dp, mp), P(mp, dp), P(mp, dp))
    return jax.shard_map(
        on_device, mesh=fine, in_specs=in_specs, out_specs=out_specs, check_vma=False
    )
```

```python
import jax
import jax.numpy as jnp
from jax import lax
from jax.experimental import pallas as pl
from jax.experimental.pallas import tpu as pltpu
from jax.sharding import Mesh, PartitionSpec as P

beta_one = 0.95
beta_two = 0.95
bias_one = 1.0 - 0.95**10
bias_two = 1.0 - 0.95**10
epsilon = 1e-08

XY = ("x", "y")
ZC = ("zl", "zh", "core")
NEAR = (0, -1, 1, 2)
BLOCK = 1024
ROWS = 256
VMEM_LIMIT = 32 * 1024 * 1024


def shift(value, axis, by):
    return lax.ppermute(value, axis, [(i, (i + by) % 4) for i in range(4)])


def line_gather(shard, zl):
    held = [shard] + [shift(shard, "zl", t) for t in (1, 2, 3)]
    ordered = []
    for at in range(4):
        back = (zl - at) & 3
        ordered.append(
            jnp.where(
                back < 2,
                jnp.where(back == 0, held[0], held[1]),
                jnp.where(back == 2, held[2], held[3]),
            )
        )
    return jnp.stack(ordered, axis=-3).reshape(*shard.shape[:-2], 64, BLOCK)


def ring(axis, shard_for):
    return [shard_for(0)] + [shift(shard_for(by), axis, by) for by in (1, -1, 2)]


def first_kernel(place, kept, given, *refs):
    pieces, (sent, whole) = refs[:8], refs[8:]
    x, y, core = place[0], place[1], place[3]
    step = pl.program_id(0)

    @pl.when(step == 0)
    def _():
        for half in range(2):
            for outer in range(4):
                for inner in range(4):
                    to_x, to_y = (inner, outer) if half == 0 else (outer, inner)
                    chip = ((x + NEAR[to_x] + 4) & 3) * 4 + ((y + NEAR[to_y] + 4) & 3)
                    row = pl.multiple_of(chip * 64 + half * 32, 32)
                    whole[pl.ds(row, 32), :] = pieces[4 * half + outer][inner]

    rows = jnp.where(step == 0, kept[...], given[...])
    turned = jnp.dot(rows, whole[...], preferred_element_type=jnp.float32)
    turned = turned.astype(jnp.bfloat16).T
    for low in range(2):
        sent[low ^ core, :, 0] = turned[512 * low : 512 * low + 512].reshape(16, 32, ROWS)


def first_stage(place, kept, given, pieces):
    return pl.pallas_call(
        first_kernel,
        out_shape=jax.ShapeDtypeStruct((2, 16, 2, 32, ROWS), jnp.bfloat16),
        grid_spec=pltpu.PrefetchScalarGridSpec(
            num_scalar_prefetch=1,
            grid=(2,),
            in_specs=[pl.BlockSpec((ROWS, BLOCK), lambda g, place: (0, 0))] * 2
            + [pl.BlockSpec((4, 32, BLOCK), lambda g, place: (0, 0, 0))] * len(pieces),
            out_specs=pl.BlockSpec(
                (2, 16, 1, 32, ROWS), lambda g, place: (0, 0, (place[0] >> 1) ^ g, 0, 0)
            ),
            scratch_shapes=[pltpu.VMEM((BLOCK, BLOCK), jnp.bfloat16)],
        ),
        compiler_params=pltpu.CompilerParams(vmem_limit_bytes=VMEM_LIMIT),
        cost_estimate=pl.CostEstimate(
            flops=2 * ROWS * 2 * BLOCK * BLOCK, bytes_accessed=4 * 2**20, transcendentals=0
        ),
        name="rotate_columns",
    )(place, kept, given, *pieces)


def middle_kernel(place, owned, left_block, first, second, back, first_out, second_out):
    left = left_block[:, 0].reshape(BLOCK, BLOCK)
    low = place[0] & 1
    columns = jnp.concatenate(
        [
            jnp.concatenate(
                [owned[0, 4 * z + (q & 2) + ((q & 1) ^ low)] for q in range(4)], axis=0
            )
            for z in range(4)
        ],
        axis=1,
    )
    eigen_grad = jnp.dot(columns, left, preferred_element_type=jnp.float32).T
    first_new = beta_one * first[...] + (1.0 - beta_one) * eigen_grad
    second_new = beta_two * second[...] + (1.0 - beta_two) * eigen_grad * eigen_grad
    first_out[...] = first_new
    second_out[...] = second_new
    direction = first_new / bias_one / (jnp.sqrt(second_new / bias_two) + epsilon)
    turned = lax.dot_general(
        direction.astype(jnp.bfloat16).T,
        left,
        (((1,), (1,)), ((), ())),
        preferred_element_type=jnp.float32,
    ).astype(jnp.bfloat16)
    for z in range(4):
        back[4 * z : 4 * z + 4, 0] = turned[:, z * ROWS : (z + 1) * ROWS].reshape(4, 32, ROWS)


def middle_stage(place, owned, left_whole, first_moment, second_moment):
    pieces = pl.BlockSpec((16, 1, 32, ROWS), lambda b, place: (0, b, 0, 0))
    moments = pl.BlockSpec((BLOCK, 128), lambda b, place: (b, 0))
    return pl.pallas_call(
        middle_kernel,
        out_shape=(
            jax.ShapeDtypeStruct((16, 4, 32, ROWS), jnp.bfloat16),
            jax.ShapeDtypeStruct((4 * BLOCK, 128), jnp.float32),
            jax.ShapeDtypeStruct((4 * BLOCK, 128), jnp.float32),
        ),
        grid_spec=pltpu.PrefetchScalarGridSpec(
            num_scalar_prefetch=1,
            grid=(4,),
            in_specs=[
                pl.BlockSpec((1, 16, 32, ROWS), lambda b, place: (b, 0, 0, 0)),
                pl.BlockSpec((16, 1, 64, BLOCK), lambda b, place: (0, b, 0, 0)),
                moments,
                moments,
            ],
            out_specs=(pieces, moments, moments),
        ),
        compiler_params=pltpu.CompilerParams(vmem_limit_bytes=VMEM_LIMIT),
        cost_estimate=pl.CostEstimate(
            flops=4 * 4 * BLOCK * BLOCK * 128,
            bytes_accessed=18 * 2**20,
            transcendentals=4 * BLOCK * 128,
        ),
        name="moments_and_direction",
    )(place, owned, left_whole, first_moment, second_moment)


def last_kernel(back, right_whole, update):
    update[...] = lax.dot_general(
        back[...].reshape(BLOCK, ROWS).T,
        right_whole[:, 0].reshape(BLOCK // 2, BLOCK),
        (((1,), (1,)), ((), ())),
        preferred_element_type=jnp.float32,
    )


def last_stage(back, right_whole):
    return pl.pallas_call(
        last_kernel,
        out_shape=jax.ShapeDtypeStruct((ROWS, 2 * BLOCK), jnp.float32),
        grid=(2, 2),
        in_specs=[
            pl.BlockSpec((8, 128, ROWS), lambda k, i: (k, 0, 0)),
            pl.BlockSpec((8, 1, 64, BLOCK), lambda k, i: (i, k, 0, 0)),
        ],
        out_specs=pl.BlockSpec((ROWS, BLOCK // 2), lambda k, i: (0, 2 * k + i)),
        compiler_params=pltpu.CompilerParams(vmem_limit_bytes=VMEM_LIMIT),
        cost_estimate=pl.CostEstimate(
            flops=2 * ROWS * 2 * BLOCK * BLOCK, bytes_accessed=7 * 2**20, transcendentals=0
        ),
        name="rotate_back_columns",
    )(back, right_whole)


def gather_whole(line):
    whole = lax.all_gather(line.reshape(-1, BLOCK), XY, axis=0, tiled=True)
    return whole.reshape(16, *line.shape)


def on_device(grad, right_basis, left_basis, first_moment, second_moment):
    x, y, zl, core = (
        lax.axis_index(axis).astype(jnp.int32) for axis in ("x", "y", "zl", "core")
    )
    place = jnp.stack([x, y, zl, core])
    tie = lax.optimization_barrier

    def for_x(by, blocks):
        return jnp.where(((x + by) & 3) < 2, blocks[0], blocks[1])

    halves = grad[:, :BLOCK], grad[:, BLOCK:]
    kept = for_x(0, halves)
    given = lax.ppermute(for_x(2, halves), "x", [(i, i ^ 2) for i in range(4)])

    line = line_gather(jnp.concatenate([right_basis, left_basis]), zl)
    given, line = tie((given, line))
    left_whole = gather_whole(line[2:])
    right = line[0], line[1]
    by_x = jnp.stack(ring("x", lambda by: for_x(by, [block[:32] for block in right])))
    both = jnp.stack([block[32:] for block in right])
    by_y = jnp.stack(ring("y", lambda by: both))
    by_x, by_y = tie((by_x, by_y))
    pieces = ring("y", lambda by: by_x) + ring("x", lambda by: for_x(by, (by_y[:, 0], by_y[:, 1])))
    sent = first_stage(place, kept, given, pieces)

    moved = []
    for t in range(2):
        pairs = [
            (4 * high + 2 * low + c, 4 * high + 2 * (c ^ t) + low)
            for high in range(2)
            for low in range(2)
            for c in range(2)
        ]
        moved.append(lax.ppermute(sent[t], ("x", "core"), pairs))
    moved = jnp.stack(moved, axis=2).reshape(32, 64, ROWS)
    owned = lax.all_to_all(moved, ("y", "zl", "zh"), split_axis=0, concat_axis=0, tiled=True)
    owned = owned.reshape(4, 16, 32, ROWS)
    owned, right_line = tie((owned, line[:2]))
    right_whole = gather_whole(right_line)
    left_whole, first_moment, second_moment = (
        pltpu.with_memory_space_constraint(value, pltpu.HBM)
        for value in (left_whole, first_moment, second_moment)
    )
    back, first_new, second_new = middle_stage(
        place, owned, left_whole, first_moment, second_moment
    )
    back = lax.all_to_all(
        back.reshape(16, 128, ROWS), ZC, split_axis=0, concat_axis=0, tiled=True
    )
    back = back.reshape(4, 4, 4, 32, ROWS).transpose(1, 2, 0, 3, 4).reshape(16, 128, ROWS)
    back = lax.all_to_all(back, XY, split_axis=0, concat_axis=0, tiled=True)
    return last_stage(back, right_whole), first_new, second_new


def solution(mesh):
    fine = Mesh(mesh.devices.reshape(4, 4, 4, 2, 2), ("x", "y", "zl", "zh", "core"))
    dp, mp = ("x", "y", "zl"), ("zh", "core")
    in_specs = (P(dp, mp), P(mp, dp, None), P(mp, dp, None), P(mp, dp), P(mp, dp))
    out_specs = (P(dp, mp), P(mp, dp), P(mp, dp))
    return jax.shard_map(
        on_device, mesh=fine, in_specs=in_specs, out_specs=out_specs, check_vma=False
    )
```

```python
import jax
import jax.numpy as jnp
from jax import lax
from jax.experimental import pallas as pl
from jax.experimental.pallas import tpu as pltpu
from jax.sharding import Mesh, PartitionSpec as P

beta_one = 0.95
beta_two = 0.95
bias_one = 1.0 - 0.95**10
bias_two = 1.0 - 0.95**10
epsilon = 1e-08

XY = ("x", "y")
ZC = ("zl", "zh", "core")
NEAR = (0, -1, 1, 2)
BLOCK = 1024
ROWS = 256
VMEM_LIMIT = 32 * 1024 * 1024


def shift(value, axis, by):
    return lax.ppermute(value, axis, [(i, (i + by) % 4) for i in range(4)])


def line_gather(shard, zl):
    held = [shard] + [shift(shard, "zl", t) for t in (1, 2, 3)]
    ordered = []
    for at in range(4):
        back = (zl - at) & 3
        ordered.append(
            jnp.where(
                back < 2,
                jnp.where(back == 0, held[0], held[1]),
                jnp.where(back == 2, held[2], held[3]),
            )
        )
    return jnp.stack(ordered, axis=-3).reshape(*shard.shape[:-2], 64, BLOCK)


def ring(axis, shard_for):
    return [shard_for(0)] + [shift(shard_for(by), axis, by) for by in (1, -1, 2)]


def first_kernel(place, kept, given, *refs):
    pieces, (sent, whole) = refs[:8], refs[8:]
    x, y, core = place[0], place[1], place[3]
    step = pl.program_id(0)

    @pl.when(step == 0)
    def _():
        for half in range(2):
            for outer in range(4):
                for inner in range(4):
                    to_x, to_y = (inner, outer) if half == 0 else (outer, inner)
                    chip = ((x + NEAR[to_x] + 4) & 3) * 4 + ((y + NEAR[to_y] + 4) & 3)
                    row = pl.multiple_of(chip * 64 + half * 32, 32)
                    whole[pl.ds(row, 32), :] = pieces[4 * half + outer][inner]

    rows = jnp.where(step == 0, kept[...], given[...])
    turned = jnp.dot(rows, whole[...], preferred_element_type=jnp.float32)
    turned = turned.astype(jnp.bfloat16).T
    for low in range(2):
        sent[low ^ core, :, 0] = turned[512 * low : 512 * low + 512].reshape(16, 32, ROWS)


def first_stage(place, kept, given, pieces):
    return pl.pallas_call(
        first_kernel,
        out_shape=jax.ShapeDtypeStruct((2, 16, 2, 32, ROWS), jnp.bfloat16),
        grid_spec=pltpu.PrefetchScalarGridSpec(
            num_scalar_prefetch=1,
            grid=(2,),
            in_specs=[pl.BlockSpec((ROWS, BLOCK), lambda g, place: (0, 0))] * 2
            + [pl.BlockSpec((4, 32, BLOCK), lambda g, place: (0, 0, 0))] * len(pieces),
            out_specs=pl.BlockSpec(
                (2, 16, 1, 32, ROWS), lambda g, place: (0, 0, (place[0] >> 1) ^ g, 0, 0)
            ),
            scratch_shapes=[pltpu.VMEM((BLOCK, BLOCK), jnp.bfloat16)],
        ),
        compiler_params=pltpu.CompilerParams(vmem_limit_bytes=VMEM_LIMIT),
        cost_estimate=pl.CostEstimate(
            flops=2 * ROWS * 2 * BLOCK * BLOCK, bytes_accessed=4 * 2**20, transcendentals=0
        ),
        name="rotate_columns",
    )(place, kept, given, *pieces)


def middle_kernel(place, owned, left_block, first, second, back, first_out, second_out):
    left = left_block[:, 0].reshape(BLOCK, BLOCK)
    low = place[0] & 1
    columns = jnp.concatenate(
        [
            jnp.concatenate(
                [owned[0, 4 * z + (q & 2) + ((q & 1) ^ low)] for q in range(4)], axis=0
            )
            for z in range(4)
        ],
        axis=1,
    )
    eigen_grad = jnp.dot(columns, left, preferred_element_type=jnp.float32).T
    first_new = beta_one * first[...] + (1.0 - beta_one) * eigen_grad
    second_new = beta_two * second[...] + (1.0 - beta_two) * eigen_grad * eigen_grad
    first_out[...] = first_new
    second_out[...] = second_new
    direction = first_new / bias_one / (jnp.sqrt(second_new / bias_two) + epsilon)
    turned = (
        jnp.dot(left, direction.astype(jnp.bfloat16), preferred_element_type=jnp.float32)
        .astype(jnp.bfloat16)
        .T
    )
    for z in range(4):
        back[4 * z : 4 * z + 4, 0] = turned[:, z * ROWS : (z + 1) * ROWS].reshape(4, 32, ROWS)


def middle_stage(place, owned, left_whole, first_moment, second_moment):
    pieces = pl.BlockSpec((16, 1, 32, ROWS), lambda b, place: (0, b, 0, 0))
    moments = pl.BlockSpec((BLOCK, 128), lambda b, place: (b, 0))
    return pl.pallas_call(
        middle_kernel,
        out_shape=(
            jax.ShapeDtypeStruct((16, 4, 32, ROWS), jnp.bfloat16),
            jax.ShapeDtypeStruct((4 * BLOCK, 128), jnp.float32),
            jax.ShapeDtypeStruct((4 * BLOCK, 128), jnp.float32),
        ),
        grid_spec=pltpu.PrefetchScalarGridSpec(
            num_scalar_prefetch=1,
            grid=(4,),
            in_specs=[
                pl.BlockSpec((1, 16, 32, ROWS), lambda b, place: (b, 0, 0, 0)),
                pl.BlockSpec((16, 1, 64, BLOCK), lambda b, place: (0, b, 0, 0)),
                moments,
                moments,
            ],
            out_specs=(pieces, moments, moments),
        ),
        compiler_params=pltpu.CompilerParams(vmem_limit_bytes=VMEM_LIMIT),
        cost_estimate=pl.CostEstimate(
            flops=4 * 4 * BLOCK * BLOCK * 128,
            bytes_accessed=18 * 2**20,
            transcendentals=4 * BLOCK * 128,
        ),
        name="moments_and_direction",
    )(place, owned, left_whole, first_moment, second_moment)


def last_kernel(back, right_whole, update):
    update[...] = lax.dot_general(
        back[...].reshape(BLOCK, ROWS).T,
        right_whole[:, 0].reshape(BLOCK // 2, BLOCK),
        (((1,), (1,)), ((), ())),
        preferred_element_type=jnp.float32,
    )


def last_stage(back, right_whole):
    return pl.pallas_call(
        last_kernel,
        out_shape=jax.ShapeDtypeStruct((ROWS, 2 * BLOCK), jnp.float32),
        grid=(2, 2),
        in_specs=[
            pl.BlockSpec((8, 128, ROWS), lambda k, i: (k, 0, 0)),
            pl.BlockSpec((8, 1, 64, BLOCK), lambda k, i: (i, k, 0, 0)),
        ],
        out_specs=pl.BlockSpec((ROWS, BLOCK // 2), lambda k, i: (0, 2 * k + i)),
        compiler_params=pltpu.CompilerParams(vmem_limit_bytes=VMEM_LIMIT),
        cost_estimate=pl.CostEstimate(
            flops=2 * ROWS * 2 * BLOCK * BLOCK, bytes_accessed=7 * 2**20, transcendentals=0
        ),
        name="rotate_back_columns",
    )(back, right_whole)


def gather_whole(line):
    whole = lax.all_gather(line.reshape(-1, BLOCK), XY, axis=0, tiled=True)
    return whole.reshape(16, *line.shape)


def on_device(grad, right_basis, left_basis, first_moment, second_moment):
    x, y, zl, core = (
        lax.axis_index(axis).astype(jnp.int32) for axis in ("x", "y", "zl", "core")
    )
    place = jnp.stack([x, y, zl, core])
    tie = lax.optimization_barrier

    def for_x(by, blocks):
        return jnp.where(((x + by) & 3) < 2, blocks[0], blocks[1])

    halves = grad[:, :BLOCK], grad[:, BLOCK:]
    kept = for_x(0, halves)
    given = lax.ppermute(for_x(2, halves), "x", [(i, i ^ 2) for i in range(4)])

    both = jnp.where(
        lax.broadcasted_iota(jnp.int32, (6, 16, BLOCK), 0) < 2,
        jnp.pad(right_basis, ((0, 4), (0, 0), (0, 0))),
        jnp.pad(left_basis, ((2, 0), (0, 0), (0, 0))),
    )
    line = line_gather(both, zl)
    given, line = tie((given, line))
    left_whole = gather_whole(line[2:])
    right = line[0], line[1]
    by_x = jnp.stack(ring("x", lambda by: for_x(by, [block[:32] for block in right])))
    both = jnp.stack([block[32:] for block in right])
    by_y = jnp.stack(ring("y", lambda by: both))
    by_x, by_y = tie((by_x, by_y))
    pieces = ring("y", lambda by: by_x) + ring("x", lambda by: for_x(by, (by_y[:, 0], by_y[:, 1])))
    sent = first_stage(place, kept, given, pieces)

    moved = []
    for t in range(2):
        pairs = [
            (4 * high + 2 * low + c, 4 * high + 2 * (c ^ t) + low)
            for high in range(2)
            for low in range(2)
            for c in range(2)
        ]
        moved.append(lax.ppermute(sent[t], ("x", "core"), pairs))
    moved, right_line = tie((moved, line[:2]))
    moved = jnp.stack(moved, axis=2).reshape(32, 64, ROWS)
    owned = lax.all_to_all(moved, ("y", "zl", "zh"), split_axis=0, concat_axis=0, tiled=True)
    owned = owned.reshape(4, 16, 32, ROWS)
    right_whole = gather_whole(right_line)
    left_whole, right_whole, first_moment, second_moment = (
        pltpu.with_memory_space_constraint(value, pltpu.HBM)
        for value in (left_whole, right_whole, first_moment, second_moment)
    )
    back, first_new, second_new = middle_stage(
        place, owned, left_whole, first_moment, second_moment
    )
    back = lax.all_to_all(
        back.reshape(16, 128, ROWS), ZC, split_axis=0, concat_axis=0, tiled=True
    )
    back = back.reshape(4, 4, 4, 32, ROWS).transpose(1, 2, 0, 3, 4).reshape(16, 128, ROWS)
    back = lax.all_to_all(back, XY, split_axis=0, concat_axis=0, tiled=True)
    return last_stage(back, right_whole), first_new, second_new


def solution(mesh):
    fine = Mesh(mesh.devices.reshape(4, 4, 4, 2, 2), ("x", "y", "zl", "zh", "core"))
    dp, mp = ("x", "y", "zl"), ("zh", "core")
    in_specs = (P(dp, mp), P(mp, dp, None), P(mp, dp, None), P(mp, dp), P(mp, dp))
    out_specs = (P(dp, mp), P(mp, dp), P(mp, dp))
    return jax.shard_map(
        on_device, mesh=fine, in_specs=in_specs, out_specs=out_specs, check_vma=False
    )
```

```python
import jax
import jax.numpy as jnp
from jax import lax
from jax.experimental import pallas as pl
from jax.experimental.pallas import tpu as pltpu
from jax.sharding import Mesh, PartitionSpec as P

beta_one = 0.95
beta_two = 0.95
bias_one = 1.0 - 0.95**10
bias_two = 1.0 - 0.95**10
epsilon = 1e-08

XY = ("x", "y")
ZC = ("zh", "core", "zl")
NEAR = (0, -1, 1, 2)
BLOCK = 1024
ROWS = 256
VMEM_LIMIT = 32 * 1024 * 1024


def shift(value, axis, by):
    return lax.ppermute(value, axis, [(i, (i + by) % 4) for i in range(4)])


def line_gather(shard, zl):
    held = [shard] + [shift(shard, "zl", t) for t in (1, 2, 3)]
    ordered = []
    for at in range(4):
        back = (zl - at) & 3
        ordered.append(
            jnp.where(
                back < 2,
                jnp.where(back == 0, held[0], held[1]),
                jnp.where(back == 2, held[2], held[3]),
            )
        )
    return jnp.stack(ordered, axis=-3).reshape(*shard.shape[:-2], 64, BLOCK)


def ring(axis, shard_for):
    return [shard_for(0)] + [shift(shard_for(by), axis, by) for by in (1, -1, 2)]


def first_kernel(place, kept, given, *refs):
    pieces, (sent, whole) = refs[:8], refs[8:]
    x, y, core = place[0], place[1], place[3]
    step = pl.program_id(0)

    @pl.when(step == 0)
    def _():
        for half in range(2):
            for outer in range(4):
                for inner in range(4):
                    to_x, to_y = (inner, outer) if half == 0 else (outer, inner)
                    chip = ((x + NEAR[to_x] + 4) & 3) * 4 + ((y + NEAR[to_y] + 4) & 3)
                    row = pl.multiple_of(chip * 64 + half * 32, 32)
                    whole[pl.ds(row, 32), :] = pieces[4 * half + outer][inner]

    rows = jnp.where(step == 0, kept[...], given[...])
    turned = jnp.dot(rows, whole[...], preferred_element_type=jnp.float32)
    turned = turned.astype(jnp.bfloat16).T
    for low in range(2):
        sent[low ^ core, 0] = turned[512 * low : 512 * low + 512].reshape(16, 32, ROWS)


def first_stage(place, kept, given, pieces):
    return pl.pallas_call(
        first_kernel,
        out_shape=jax.ShapeDtypeStruct((2, 2, 16, 32, ROWS), jnp.bfloat16),
        grid_spec=pltpu.PrefetchScalarGridSpec(
            num_scalar_prefetch=1,
            grid=(2,),
            in_specs=[pl.BlockSpec((ROWS, BLOCK), lambda g, place: (0, 0))] * 2
            + [pl.BlockSpec((4, 32, BLOCK), lambda g, place: (0, 0, 0))] * len(pieces),
            out_specs=pl.BlockSpec(
                (2, 1, 16, 32, ROWS), lambda g, place: (0, (place[0] >> 1) ^ g, 0, 0, 0)
            ),
            scratch_shapes=[pltpu.VMEM((BLOCK, BLOCK), jnp.bfloat16)],
        ),
        compiler_params=pltpu.CompilerParams(vmem_limit_bytes=VMEM_LIMIT),
        cost_estimate=pl.CostEstimate(
            flops=2 * ROWS * 2 * BLOCK * BLOCK, bytes_accessed=4 * 2**20, transcendentals=0
        ),
        name="rotate_columns",
    )(place, kept, given, *pieces)


def middle_kernel(place, owned, left_block, first, second, back, first_out, second_out):
    left = left_block[:, 0].reshape(BLOCK, BLOCK)
    low = place[0] & 1
    columns = jnp.concatenate(
        [
            jnp.concatenate(
                [owned[q >> 1, 0, 2 * z + ((q & 1) ^ low)] for q in range(4)], axis=0
            )
            for z in range(4)
        ],
        axis=1,
    )
    eigen_grad = jnp.dot(columns, left, preferred_element_type=jnp.float32).T
    first_new = beta_one * first[...] + (1.0 - beta_one) * eigen_grad
    second_new = beta_two * second[...] + (1.0 - beta_two) * eigen_grad * eigen_grad
    first_out[...] = first_new
    second_out[...] = second_new
    direction = first_new / bias_one / (jnp.sqrt(second_new / bias_two) + epsilon)
    turned = (
        jnp.dot(left, direction.astype(jnp.bfloat16), preferred_element_type=jnp.float32)
        .astype(jnp.bfloat16)
        .T
    )
    for z in range(4):
        for q in range(4):
            back[4 * q + z, 0] = turned[32 * q : 32 * q + 32, z * ROWS : (z + 1) * ROWS]


def middle_stage(place, owned, left_whole, first_moment, second_moment):
    pieces = pl.BlockSpec((16, 1, 32, ROWS), lambda b, place: (0, b, 0, 0))
    moments = pl.BlockSpec((BLOCK, 128), lambda b, place: (b, 0))
    return pl.pallas_call(
        middle_kernel,
        out_shape=(
            jax.ShapeDtypeStruct((16, 4, 32, ROWS), jnp.bfloat16),
            jax.ShapeDtypeStruct((4 * BLOCK, 128), jnp.float32),
            jax.ShapeDtypeStruct((4 * BLOCK, 128), jnp.float32),
        ),
        grid_spec=pltpu.PrefetchScalarGridSpec(
            num_scalar_prefetch=1,
            grid=(4,),
            in_specs=[
                pl.BlockSpec((2, 1, 8, 32, ROWS), lambda b, place: (0, b, 0, 0, 0)),
                pl.BlockSpec((16, 1, 64, BLOCK), lambda b, place: (0, b, 0, 0)),
                moments,
                moments,
            ],
            out_specs=(pieces, moments, moments),
        ),
        compiler_params=pltpu.CompilerParams(vmem_limit_bytes=VMEM_LIMIT),
        cost_estimate=pl.CostEstimate(
            flops=4 * 4 * BLOCK * BLOCK * 128,
            bytes_accessed=18 * 2**20,
            transcendentals=4 * BLOCK * 128,
        ),
        name="moments_and_direction",
    )(place, owned, left_whole, first_moment, second_moment)


def last_kernel(back, right_whole, update):
    update[...] = lax.dot_general(
        jnp.concatenate([back[y, x] for x in range(2) for y in range(4)], axis=0).T,
        right_whole[:, 0].reshape(BLOCK // 2, BLOCK),
        (((1,), (1,)), ((), ())),
        preferred_element_type=jnp.float32,
    )


def last_stage(back, right_whole):
    return pl.pallas_call(
        last_kernel,
        out_shape=jax.ShapeDtypeStruct((ROWS, 2 * BLOCK), jnp.float32),
        grid=(2, 2),
        in_specs=[
            pl.BlockSpec((4, 2, 128, ROWS), lambda k, i: (0, k, 0, 0)),
            pl.BlockSpec((8, 1, 64, BLOCK), lambda k, i: (i, k, 0, 0)),
        ],
        out_specs=pl.BlockSpec((ROWS, BLOCK // 2), lambda k, i: (0, 2 * k + i)),
        compiler_params=pltpu.CompilerParams(vmem_limit_bytes=VMEM_LIMIT),
        cost_estimate=pl.CostEstimate(
            flops=2 * ROWS * 2 * BLOCK * BLOCK, bytes_accessed=7 * 2**20, transcendentals=0
        ),
        name="rotate_back_columns",
    )(back, right_whole)


def gather_whole(line):
    whole = lax.all_gather(line.reshape(-1, BLOCK), XY, axis=0, tiled=True)
    return whole.reshape(16, *line.shape)


def on_device(grad, right_basis, left_basis, first_moment, second_moment):
    x, y, zl, core = (
        lax.axis_index(axis).astype(jnp.int32) for axis in ("x", "y", "zl", "core")
    )
    place = jnp.stack([x, y, zl, core])
    tie = lax.optimization_barrier

    def for_x(by, blocks):
        return jnp.where(((x + by) & 3) < 2, blocks[0], blocks[1])

    halves = grad[:, :BLOCK], grad[:, BLOCK:]
    kept = for_x(0, halves)
    given = lax.ppermute(for_x(2, halves), "x", [(i, i ^ 2) for i in range(4)])

    both = jnp.where(
        lax.broadcasted_iota(jnp.int32, (6, 16, BLOCK), 0) < 2,
        jnp.pad(right_basis, ((0, 4), (0, 0), (0, 0))),
        jnp.pad(left_basis, ((2, 0), (0, 0), (0, 0))),
    )
    line = line_gather(both, zl)
    given, line = tie((given, line))
    left_whole = gather_whole(line[2:])
    right = line[0], line[1]
    by_x = jnp.stack(ring("x", lambda by: for_x(by, [block[:32] for block in right])))
    both = jnp.stack([block[32:] for block in right])
    by_y = jnp.stack(ring("y", lambda by: both))
    by_x, by_y = tie((by_x, by_y))
    pieces = ring("y", lambda by: by_x) + ring("x", lambda by: for_x(by, (by_y[:, 0], by_y[:, 1])))
    sent = first_stage(place, kept, given, pieces)

    moved = []
    for t in range(2):
        pairs = [
            (4 * high + 2 * low + c, 4 * high + 2 * (c ^ t) + low)
            for high in range(2)
            for low in range(2)
            for c in range(2)
        ]
        moved.append(lax.ppermute(sent[t], ("x", "core"), pairs))
    moved, right_line = tie((moved, line[:2]))
    moved = jnp.stack(moved, axis=2).reshape(32, 64, ROWS)
    owned = lax.all_to_all(moved, ("zh", "y", "zl"), split_axis=0, concat_axis=0, tiled=True)
    owned = owned.reshape(2, 4, 8, 32, ROWS)
    right_whole = gather_whole(right_line)
    left_whole, right_whole, first_moment, second_moment = (
        pltpu.with_memory_space_constraint(value, pltpu.HBM)
        for value in (left_whole, right_whole, first_moment, second_moment)
    )
    back, first_new, second_new = middle_stage(
        place, owned, left_whole, first_moment, second_moment
    )
    back = lax.all_to_all(
        back.reshape(16, 128, ROWS), ZC, split_axis=0, concat_axis=0, tiled=True
    )
    back = back.reshape(4, 4, 4, 32, ROWS).transpose(2, 0, 1, 3, 4).reshape(16, 128, ROWS)
    back = lax.all_to_all(back, ("y", "x"), split_axis=0, concat_axis=0, tiled=True)
    back = back.reshape(4, 4, 128, ROWS)
    return last_stage(back, right_whole), first_new, second_new


def solution(mesh):
    fine = Mesh(mesh.devices.reshape(4, 4, 4, 2, 2), ("x", "y", "zl", "zh", "core"))
    dp, mp = ("x", "y", "zl"), ("zh", "core")
    in_specs = (P(dp, mp), P(mp, dp, None), P(mp, dp, None), P(mp, dp), P(mp, dp))
    out_specs = (P(dp, mp), P(mp, dp), P(mp, dp))
    return jax.shard_map(
        on_device, mesh=fine, in_specs=in_specs, out_specs=out_specs, check_vma=False
    )
```

```python
import jax
import jax.numpy as jnp
from jax import lax
from jax.experimental import pallas as pl
from jax.experimental.pallas import tpu as pltpu
from jax.sharding import Mesh, PartitionSpec as P

beta_one = 0.95
beta_two = 0.95
bias_one = 1.0 - 0.95**10
bias_two = 1.0 - 0.95**10
epsilon = 1e-08

XY = ("x", "y")
ZC = ("zl", "zh", "core")
NEAR = (0, -1, 1, 2)
BLOCK = 1024
ROWS = 256
VMEM_LIMIT = 32 * 1024 * 1024


def shift(value, axis, by):
    return lax.ppermute(value, axis, [(i, (i + by) % 4) for i in range(4)])


def line_gather(shard, zl):
    held = [shard] + [shift(shard, "zl", t) for t in (1, 2, 3)]
    ordered = []
    for at in range(4):
        back = (zl - at) & 3
        ordered.append(
            jnp.where(
                back < 2,
                jnp.where(back == 0, held[0], held[1]),
                jnp.where(back == 2, held[2], held[3]),
            )
        )
    return jnp.stack(ordered, axis=-3).reshape(*shard.shape[:-2], 64, BLOCK)


def ring(axis, shard_for):
    return [shard_for(0)] + [shift(shard_for(by), axis, by) for by in (1, -1, 2)]


def first_kernel(place, kept, given, *refs):
    pieces, (sent, whole) = refs[:8], refs[8:]
    x, y, core = place[0], place[1], place[3]
    step = pl.program_id(0)

    @pl.when(step == 0)
    def _():
        for half in range(2):
            for outer in range(4):
                for inner in range(4):
                    to_x, to_y = (inner, outer) if half == 0 else (outer, inner)
                    chip = ((x + NEAR[to_x] + 4) & 3) * 4 + ((y + NEAR[to_y] + 4) & 3)
                    row = pl.multiple_of(chip * 64 + half * 32, 32)
                    whole[pl.ds(row, 32), :] = pieces[4 * half + outer][inner]

    rows = jnp.where(step == 0, kept[...], given[...])
    turned = jnp.dot(rows, whole[...], preferred_element_type=jnp.float32)
    turned = turned.astype(jnp.bfloat16).T
    for low in range(2):
        sent[low ^ core, :, 0] = turned[512 * low : 512 * low + 512].reshape(16, 32, ROWS)


def first_stage(place, kept, given, pieces):
    return pl.pallas_call(
        first_kernel,
        out_shape=jax.ShapeDtypeStruct((2, 16, 2, 32, ROWS), jnp.bfloat16),
        grid_spec=pltpu.PrefetchScalarGridSpec(
            num_scalar_prefetch=1,
            grid=(2,),
            in_specs=[pl.BlockSpec((ROWS, BLOCK), lambda g, place: (0, 0))] * 2
            + [pl.BlockSpec((4, 32, BLOCK), lambda g, place: (0, 0, 0))] * len(pieces),
            out_specs=pl.BlockSpec(
                (2, 16, 1, 32, ROWS), lambda g, place: (0, 0, (place[0] >> 1) ^ g, 0, 0)
            ),
            scratch_shapes=[pltpu.VMEM((BLOCK, BLOCK), jnp.bfloat16)],
        ),
        compiler_params=pltpu.CompilerParams(vmem_limit_bytes=VMEM_LIMIT),
        cost_estimate=pl.CostEstimate(
            flops=2 * ROWS * 2 * BLOCK * BLOCK, bytes_accessed=4 * 2**20, transcendentals=0
        ),
        name="rotate_columns",
    )(place, kept, given, *pieces)


def middle_kernel(place, owned, left_block, first, second, back, first_out, second_out):
    left = jnp.concatenate([left_block[y, x, 0] for x in range(4) for y in range(4)], axis=0)
    low = place[0] & 1
    columns = jnp.concatenate(
        [
            jnp.concatenate(
                [owned[0, 4 * z + (q & 2) + ((q & 1) ^ low)] for q in range(4)], axis=0
            )
            for z in range(4)
        ],
        axis=1,
    )
    eigen_grad = jnp.dot(columns, left, preferred_element_type=jnp.float32).T
    first_new = beta_one * first[...] + (1.0 - beta_one) * eigen_grad
    second_new = beta_two * second[...] + (1.0 - beta_two) * eigen_grad * eigen_grad
    first_out[...] = first_new
    second_out[...] = second_new
    direction = first_new / bias_one / (jnp.sqrt(second_new / bias_two) + epsilon)
    turned = (
        jnp.dot(left, direction.astype(jnp.bfloat16), preferred_element_type=jnp.float32)
        .astype(jnp.bfloat16)
        .T
    )
    for z in range(4):
        back[4 * z : 4 * z + 4, 0] = turned[:, z * ROWS : (z + 1) * ROWS].reshape(4, 32, ROWS)


def middle_stage(place, owned, left_whole, first_moment, second_moment):
    pieces = pl.BlockSpec((16, 1, 32, ROWS), lambda b, place: (0, b, 0, 0))
    moments = pl.BlockSpec((BLOCK, 128), lambda b, place: (b, 0))
    return pl.pallas_call(
        middle_kernel,
        out_shape=(
            jax.ShapeDtypeStruct((16, 4, 32, ROWS), jnp.bfloat16),
            jax.ShapeDtypeStruct((4 * BLOCK, 128), jnp.float32),
            jax.ShapeDtypeStruct((4 * BLOCK, 128), jnp.float32),
        ),
        grid_spec=pltpu.PrefetchScalarGridSpec(
            num_scalar_prefetch=1,
            grid=(4,),
            in_specs=[
                pl.BlockSpec((1, 16, 32, ROWS), lambda b, place: (b, 0, 0, 0)),
                pl.BlockSpec((4, 4, 1, 64, BLOCK), lambda b, place: (0, 0, b, 0, 0)),
                moments,
                moments,
            ],
            out_specs=(pieces, moments, moments),
        ),
        compiler_params=pltpu.CompilerParams(vmem_limit_bytes=VMEM_LIMIT),
        cost_estimate=pl.CostEstimate(
            flops=4 * 4 * BLOCK * BLOCK * 128,
            bytes_accessed=18 * 2**20,
            transcendentals=4 * BLOCK * 128,
        ),
        name="moments_and_direction",
    )(place, owned, left_whole, first_moment, second_moment)


def last_kernel(back, right_whole, update):
    update[...] = lax.dot_general(
        back[...].reshape(BLOCK, ROWS).T,
        jnp.concatenate([right_whole[y, x, 0] for x in range(2) for y in range(4)], axis=0),
        (((1,), (1,)), ((), ())),
        preferred_element_type=jnp.float32,
    )


def last_stage(back, right_whole):
    return pl.pallas_call(
        last_kernel,
        out_shape=jax.ShapeDtypeStruct((ROWS, 2 * BLOCK), jnp.float32),
        grid=(2, 2),
        in_specs=[
            pl.BlockSpec((8, 128, ROWS), lambda k, i: (k, 0, 0)),
            pl.BlockSpec((4, 2, 1, 64, BLOCK), lambda k, i: (0, i, k, 0, 0)),
        ],
        out_specs=pl.BlockSpec((ROWS, BLOCK // 2), lambda k, i: (0, 2 * k + i)),
        compiler_params=pltpu.CompilerParams(vmem_limit_bytes=VMEM_LIMIT),
        cost_estimate=pl.CostEstimate(
            flops=2 * ROWS * 2 * BLOCK * BLOCK, bytes_accessed=7 * 2**20, transcendentals=0
        ),
        name="rotate_back_columns",
    )(back, right_whole)


def gather_whole(line):
    whole = lax.all_gather(line.reshape(-1, BLOCK), ("y", "x"), axis=0, tiled=True)
    return whole.reshape(4, 4, *line.shape)


def on_device(grad, right_basis, left_basis, first_moment, second_moment):
    x, y, zl, core = (
        lax.axis_index(axis).astype(jnp.int32) for axis in ("x", "y", "zl", "core")
    )
    place = jnp.stack([x, y, zl, core])
    tie = lax.optimization_barrier

    def for_x(by, blocks):
        return jnp.where(((x + by) & 3) < 2, blocks[0], blocks[1])

    halves = grad[:, :BLOCK], grad[:, BLOCK:]
    kept = for_x(0, halves)
    given = lax.ppermute(for_x(2, halves), "x", [(i, i ^ 2) for i in range(4)])

    both = jnp.where(
        lax.broadcasted_iota(jnp.int32, (6, 16, BLOCK), 0) < 2,
        jnp.pad(right_basis, ((0, 4), (0, 0), (0, 0))),
        jnp.pad(left_basis, ((2, 0), (0, 0), (0, 0))),
    )
    line = line_gather(both, zl)
    given, line = tie((given, line))
    left_whole = gather_whole(line[2:])
    right = line[0], line[1]
    by_x = jnp.stack(ring("x", lambda by: for_x(by, [block[:32] for block in right])))
    both = jnp.stack([block[32:] for block in right])
    by_y = jnp.stack(ring("y", lambda by: both))
    by_x, by_y = tie((by_x, by_y))
    pieces = ring("y", lambda by: by_x) + ring("x", lambda by: for_x(by, (by_y[:, 0], by_y[:, 1])))
    sent = first_stage(place, kept, given, pieces)

    moved = []
    for t in range(2):
        pairs = [
            (4 * high + 2 * low + c, 4 * high + 2 * (c ^ t) + low)
            for high in range(2)
            for low in range(2)
            for c in range(2)
        ]
        moved.append(lax.ppermute(sent[t], ("x", "core"), pairs))
    moved, right_line = tie((moved, line[:2]))
    moved = jnp.stack(moved, axis=2).reshape(32, 64, ROWS)
    owned = lax.all_to_all(moved, ("y", "zl", "zh"), split_axis=0, concat_axis=0, tiled=True)
    owned = owned.reshape(4, 16, 32, ROWS)
    right_whole = gather_whole(right_line)
    left_whole, right_whole, first_moment, second_moment = (
        pltpu.with_memory_space_constraint(value, pltpu.HBM)
        for value in (left_whole, right_whole, first_moment, second_moment)
    )
    back, first_new, second_new = middle_stage(
        place, owned, left_whole, first_moment, second_moment
    )
    back = lax.all_to_all(
        back.reshape(16, 128, ROWS), ZC, split_axis=0, concat_axis=0, tiled=True
    )
    back = back.reshape(4, 4, 4, 32, ROWS).transpose(1, 2, 0, 3, 4).reshape(16, 128, ROWS)
    back = lax.all_to_all(back, XY, split_axis=0, concat_axis=0, tiled=True)
    return last_stage(back, right_whole), first_new, second_new


def solution(mesh):
    fine = Mesh(mesh.devices.reshape(4, 4, 4, 2, 2), ("x", "y", "zl", "zh", "core"))
    dp, mp = ("x", "y", "zl"), ("zh", "core")
    in_specs = (P(dp, mp), P(mp, dp, None), P(mp, dp, None), P(mp, dp), P(mp, dp))
    out_specs = (P(dp, mp), P(mp, dp), P(mp, dp))
    return jax.shard_map(
        on_device, mesh=fine, in_specs=in_specs, out_specs=out_specs, check_vma=False
    )
```
